512 devices in a mesh: blk: 16 (over z_lo, x), head: 32 (over y, z_hi, core).
Axes of the slice: x: 4, y: 8, z: 8 (z_hi: 2, z_lo: 4; z = z_hi * 4 + z_lo), core: 2. Of those that a mesh axis runs over, the one named last changes fastest.
Arguments:
- queries: bfloat16 [32768, 12288], P(('blk', 'head')), may hold values from -64 to 64, as said below
- exponents: int32 [32768, 64], P(('blk', 'head')), may hold values from -2 to 2
- latent: bfloat16 [32768, 576], P(('blk', 'head')), may hold values from -6 to 6, as said below
- segments: int32 [32768], P(('blk', 'head')), may hold values from 0 to 47, never falling along the last dimension, each value on 1 to 1024 neighbouring positions
- key_weight: bfloat16 [512, 8192], P(None, 'head'), may hold values from -0.25 to 0.25
- value_weight: bfloat16 [512, 8192], P(None, 'head'), may hold values from -0.25 to 0.25
Outputs:
- attended: bfloat16 [32768, 8192], P(('blk', 'head'))
The draws below stay inside these ranges and needn't reach their ends.
Inputs may be any that keep to these rules, and one draw needn't show every extreme that they name: queries stay within the range. `latent`: latents stay within the range. `segments`: document numbers never fall along the sequence, and a document holds at most 1024 tokens.
All inputs are finite; a program needn't handle non-finite values.
Results may differ from the reference program's by a relative error of at most 0.0069.
Values may be sent and summed in bfloat16 or wider, within the bound.
A program may use at most 64 MiB of HBM per device.

```python
import math
import jax
import jax.numpy as jnp
import numpy as np
from jax import lax

HEADS = 64
NOPE = 128
ROPE = 64
LATENT = 512
VDIM = 128
TOKENS = 32768
MOST = 1024
BLOCK = 512
LEAD = 1024
N_BLK = 16


def latent_base(key):
    return jnp.clip(jax.random.normal(jax.random.fold_in(key, 11), (TOKENS, LATENT + ROPE), jnp.float32), -6.0, 6.0)


def draw_latent(key, part):
    return latent_base(key).astype(jnp.bfloat16)


def draw_queries(key, part):
    base = jax.random.normal(jax.random.fold_in(key, 23), (TOKENS, HEADS, NOPE + ROPE), jnp.float32)
    base = jnp.clip(base, -6.0, 6.0)
    return base.reshape(TOKENS, HEADS * (NOPE + ROPE)).astype(jnp.bfloat16)


def touch_ends(drawn, rng, low, high):
    longest = drawn.shape.index(max(drawn.shape))
    spots = []
    for shift in (0, 1):
        where = [jax.random.randint(jax.random.fold_in(rng, axis), (), 0, length) for axis, length in enumerate(drawn.shape)]
        where[longest] = (where[longest] + shift) % drawn.shape[longest]
        spots.append(tuple(where))
    return drawn.at[spots[0]].set(low).at[spots[1]].set(high)


def levels(key, dims, cuts, low, top_value):
    level, own = 1.0, jax.random.fold_in(key, 6)
    for dim, blocks in cuts:
        steps = jnp.exp(jax.random.uniform(jax.random.fold_in(own, dim), (blocks,), jnp.float32, low / len(cuts), top_value / len(cuts)))
        level = level * jnp.repeat(steps, dims[dim] // blocks).reshape([-1 if axis == dim else 1 for axis in range(len(dims))])
    return level


def length_profile(number_of, total, bound, slope):
    portions = [(1 << 20) // math.isqrt(standing ** slope) + 1 for standing in range(2, number_of + 1)]
    rest, holding = total - bound - (number_of - 1), [1] * (number_of - 1)
    while rest > 0:
        candidates = [i for i in range(number_of - 1) if holding[i] < bound]
        pool, left = sum([portions[i] for i in candidates]), rest
        for i in candidates:
            extra = min(bound - holding[i], max(1, left * portions[i] // pool), rest)
            holding[i] = holding[i] + extra
            rest = rest - extra
    return np.array([bound] + holding)


def uneven(key, number_of, total, bound, slope):
    if number_of == 2:
        one = jax.random.randint(key, (), max(1, total - bound), min(bound, total - 1) + 1)
        return jnp.stack([one, total - one])
    tallies = jnp.asarray(length_profile(number_of, total, bound, slope), jnp.int32)
    couples = (number_of - 1) // 2
    giver, sink = tallies[1:1 + 2 * couples:2], tallies[2:2 + 2 * couples:2]
    margin = jnp.minimum(giver - 1, bound - sink)
    passed = jax.random.randint(jax.random.fold_in(key, 1), (couples,), 0, 1 << 20) % (margin + 1)
    tallies = tallies.at[1:1 + 2 * couples:2].set(giver - passed).at[2:2 + 2 * couples:2].set(sink + passed)
    return tallies[jax.random.permutation(jax.random.fold_in(key, 2), number_of)]


def bell_draw(key, dims, width, reach, pieces=(), kind=jnp.bfloat16):
    level = levels(key, dims, pieces, -0.22, 0.18) if pieces else 1.0
    values = jax.random.normal(key, dims, jnp.float32) * width * level
    return jnp.minimum(jnp.maximum(values, -reach), reach).astype(kind)


def setup_inputs(seed: int = 0) -> dict:
    splits = jax.random.split(jax.random.key(seed), 7)
    queries = draw_queries(jax.random.fold_in(splits[6], 71), 0)
    exponents = touch_ends(jax.random.randint(splits[1], (TOKENS, HEADS), -2, 3), jax.random.fold_in(splits[1], 1), -2, 2).astype(jnp.int32)
    latent = draw_latent(jax.random.fold_in(splits[6], 71), 0)
    segments = jnp.searchsorted(jnp.cumsum(uneven(splits[3], 3 * N_BLK, TOKENS, MOST, 0)), jnp.arange(TOKENS), side="right").astype(jnp.int32)
    key_weight = bell_draw(splits[4], (LATENT, HEADS * NOPE), LATENT ** -0.5, 0.25, ((1, 32),))
    value_weight = bell_draw(splits[5], (LATENT, HEADS * VDIM), LATENT ** -0.5, 0.25, ((1, 32),))
    return {"queries": queries, "exponents": exponents, "latent": latent, "segments": segments, "key_weight": key_weight, "value_weight": value_weight}


def power_two(exponent):
    result = jnp.zeros(exponent.shape, jnp.float32)
    for level in range(-4, 5):
        result = result + jnp.where(exponent == level, jnp.float32(2.0 ** level), jnp.float32(0.0))
    return result


def reference(queries, exponents, latent, segments, key_weight, value_weight):
    total = queries.shape[0]
    shaped = queries.reshape(total, HEADS, NOPE + ROPE).astype(jnp.float32)
    scaled = (shaped * power_two(exponents)[:, :, None]).astype(jnp.bfloat16)
    padded = jnp.concatenate([jnp.zeros((LEAD, LATENT + ROPE), jnp.bfloat16), latent], axis=0)
    compressed = padded[:, :LATENT]
    rope_keys = padded[:, LATENT:]
    padded_seg = jnp.concatenate([jnp.full((LEAD,), -1, jnp.int32), segments.astype(jnp.int32)], axis=0)
    padded_pos = jnp.arange(total + LEAD, dtype=jnp.int32) - LEAD
    softmax_scale = 1.0 / (NOPE + ROPE) ** 0.5
    key_heads = key_weight.reshape(LATENT, HEADS, NOPE).transpose(1, 0, 2)
    value_heads = value_weight.reshape(LATENT, HEADS, VDIM).transpose(1, 0, 2)
    query_heads = scaled.transpose(1, 0, 2)
    block_count = total // BLOCK

    def one_head(items):
        key_part, value_part, query_part = items
        keys = jnp.dot(compressed, key_part, preferred_element_type=jnp.float32).astype(jnp.bfloat16)
        values = jnp.dot(compressed, value_part, preferred_element_type=jnp.float32).astype(jnp.bfloat16)

        def one_block(index):
            start = (index * BLOCK).astype(jnp.int32)
            query_rows = lax.dynamic_slice_in_dim(query_part, start, BLOCK, 0)
            query_seg = lax.dynamic_slice_in_dim(padded_seg, start + LEAD, BLOCK, 0)
            query_pos = lax.dynamic_slice_in_dim(padded_pos, start + LEAD, BLOCK, 0)
            key_rows = lax.dynamic_slice_in_dim(keys, start, LEAD + BLOCK, 0)
            rope_rows = lax.dynamic_slice_in_dim(rope_keys, start, LEAD + BLOCK, 0)
            value_rows = lax.dynamic_slice_in_dim(values, start, LEAD + BLOCK, 0)
            key_seg = lax.dynamic_slice_in_dim(padded_seg, start, LEAD + BLOCK, 0)
            key_pos = lax.dynamic_slice_in_dim(padded_pos, start, LEAD + BLOCK, 0)
            allowed = (key_seg[None, :] == query_seg[:, None]) & (key_pos[None, :] <= query_pos[:, None]) & (key_pos[None, :] >= 0)
            scores = jnp.dot(query_rows[:, :NOPE], key_rows.T, preferred_element_type=jnp.float32)
            scores = scores + jnp.dot(query_rows[:, NOPE:], rope_rows.T, preferred_element_type=jnp.float32)
            scores = jnp.where(allowed, scores * softmax_scale, -1e30)
            largest = jnp.max(scores, axis=1, keepdims=True)
            weights = jnp.where(allowed, jnp.exp(scores - largest), 0.0)
            sums = jnp.sum(weights, axis=1, keepdims=True)
            weighted = jnp.dot(weights.astype(jnp.bfloat16), value_rows, preferred_element_type=jnp.float32)
            return (weighted / sums).astype(jnp.bfloat16)

        blocks = lax.map(one_block, jnp.arange(block_count, dtype=jnp.int32))
        return blocks.reshape(total, VDIM)

    outputs = lax.map(one_head, (key_heads, value_heads, query_heads))
    return outputs.transpose(1, 0, 2).reshape(total, HEADS * VDIM)
```

```python
import math

import jax
import jax.numpy as jnp
from jax import lax
from jax.experimental import pallas as pl
from jax.experimental.pallas import tpu as pltpu
from jax.sharding import PartitionSpec as P

NOPE = 128
ROPE = 64
LATENT = 512
VDIM = 128
WIDE = 640
ROWS = 64
CHIP = 128
WINDOW = 1152
BIG = 1e30
BF = jnp.bfloat16
F32 = jnp.float32


def kernel(
    q_ref, e_ref, lat_ref, kw_ref, vw_ref, out_ref,
    wb, q2, ev, lat, kr, obuf, pw, noth, causal,
    local_sem, sib_send, sib_recv, z_send, z_recv, lat_send, lat_recv, latsib_send, latsib_recv,
    ring_send, ring_recv, out_send, out_recv,
):
    blk = lax.axis_index("blk")
    head = lax.axis_index("head")
    n_blk = lax.axis_size("blk")
    y, zh, c = head // 4, (head // 2) % 2, head % 2

    def at(b, yy, zz, cc):
        return {"blk": b, "head": yy * 4 + zz * 2 + cc}

    sibling = at(blk, y, zh, 1 - c)
    partner = at(blk, y, 1 - zh, c)
    up = at(blk, (y + 1) % 8, zh, c)
    down = at(blk, (y + 7) % 8, zh, c)
    later = at((blk + (y + 1) // 8) % n_blk, (y + 1) % 8, zh, c)
    earlier = at((blk + n_blk - (8 - y) // 8) % n_blk, (y + 7) % 8, zh, c)

    barrier = pltpu.get_barrier_semaphore()
    for other in (sibling, partner, up, down, later, earlier):
        pl.semaphore_signal(barrier, inc=1, device_id=other)
    pl.semaphore_wait(barrier, 6)

    def remote(src, dst, send, recv, device):
        return pltpu.make_async_remote_copy(
            src_ref=src, dst_ref=dst, send_sem=send, recv_sem=recv, device_id=device
        )

    own_lat = remote(lat_ref, lat.at[4, zh, c], z_send.at[0], z_recv.at[0], partner)
    own_lat.start()
    keep_lat = pltpu.make_async_copy(lat_ref, lat.at[4, zh, c], local_sem.at[0])
    keep_lat.start()
    wk_out = remote(kw_ref, wb.at[y, zh, pl.ds(0, 512)], z_send.at[1], z_recv.at[1], partner)
    wk_out.start()
    wv_out = remote(vw_ref, wb.at[y, zh, pl.ds(512, 512)], z_send.at[2], z_recv.at[2], partner)
    wv_out.start()
    wk_keep = pltpu.make_async_copy(kw_ref, wb.at[y, zh, pl.ds(0, 512)], local_sem.at[1])
    wk_keep.start()
    wv_keep = pltpu.make_async_copy(vw_ref, wb.at[y, zh, pl.ds(512, 512)], local_sem.at[2])
    wv_keep.start()
    my_rows = pl.ds(pl.multiple_of(c * ROWS, ROWS), ROWS)
    other_rows = pl.ds(pl.multiple_of((1 - c) * ROWS, ROWS), ROWS)
    e_keep = pltpu.make_async_copy(e_ref, ev.at[my_rows], local_sem.at[3])
    e_keep.start()
    e_out = remote(e_ref, ev.at[my_rows], sib_send.at[0], sib_recv.at[0], sibling)
    e_out.start()

    def q_columns(pair):
        return pl.ds(pl.multiple_of(pair * 384, 384), 384)

    def q_start(j, carry):
        pltpu.make_async_copy(
            q_ref.at[:, q_columns(2 * j + c)], q2.at[j, my_rows], local_sem.at[4]
        ).start()
        remote(
            q_ref.at[:, q_columns(2 * j + 1 - c)], q2.at[j, my_rows],
            sib_send.at[1], sib_recv.at[1], sibling,
        ).start()
        return carry

    lax.fori_loop(0, 16, q_start, 0)

    own_lat.wait()
    keep_lat.wait()
    steps = []
    for k in range(4):
        step = remote(
            lat.at[4 - k, :, c], lat.at[3 - k, :, c], lat_send.at[k], lat_recv.at[k], later
        )
        step.start()
        share = remote(
            lat.at[4 - k, :, c], lat.at[4 - k, :, c], latsib_send.at[k], latsib_recv.at[k], sibling
        )
        share.start()
        steps.append(step)
        steps.append(share)
        if k == 0:
            wk_out.wait()
            wv_out.wait()
            wk_keep.wait()
            wv_keep.wait()
            remote(wb.at[y], wb.at[y], ring_send.at[0], ring_recv.at[0], up).start()
            remote(wb.at[y], wb.at[y], ring_send.at[4], ring_recv.at[4], down).start()
        if k == 1:
            e_keep.wait()
            e_out.wait()
            powers = jnp.zeros((CHIP, 64), F32)
            for level in range(-4, 5):
                powers = powers + jnp.where(ev[...] == level, F32(2.0**level), F32(0.0))
            pw[...] = powers.astype(BF)
            causal[...] = jnp.where(
                lax.broadcasted_iota(jnp.int32, (CHIP, CHIP), 1)
                <= lax.broadcasted_iota(jnp.int32, (CHIP, CHIP), 0),
                F32(0.0), F32(-BIG),
            )
            pltpu.make_async_copy(
                q2.at[:, my_rows], q2.at[:, my_rows], local_sem.at[4]
            ).wait()
            remote(
                q2.at[:, my_rows], q2.at[:, other_rows], sib_send.at[1], sib_recv.at[1], sibling
            ).wait()
        step.wait_recv()
    last = remote(lat.at[0, :, c], lat.at[0, :, c], latsib_send.at[4], latsib_recv.at[4], sibling)
    last.start()
    for k in range(4):
        steps[2 * k + 1].wait_recv()
    last.wait_recv()

    def chip_rows(slot):
        block = lat[slot // 2, slot % 2]
        return block.reshape(CHIP, WIDE)

    tail = jnp.concatenate(
        [chip_rows(zh + k)[:, LATENT:] for k in range(9)], axis=0
    )
    kr[0, :, NOPE:] = tail
    kr[1, :, NOPE:] = tail
    lane = lax.broadcasted_iota(jnp.int32, (CHIP, CHIP), 1)
    own_tail = chip_rows(zh + 8)[:, LATENT:].astype(F32)
    noth[...] = jnp.where(lane < ROPE, F32(0.0), (own_tail - 1.0) * F32(BIG))
    scale = F32(math.log2(math.e) / math.sqrt(NOPE + ROPE))

    def one_pair(t, carry):
        n = t // 2
        odd = n % 2
        k = (n + 1) // 2
        yy = (y + 8 + jnp.where(odd == 1, -k, k)) % 8
        zz = t % 2
        j = yy * 2 + zz
        pair = 2 * j + c

        @pl.when((zz == 0) & (odd == 1))
        def _():
            remote(wb.at[yy], wb.at[yy], ring_send.at[k - 1], ring_recv.at[k - 1], up).wait_recv()

            @pl.when(k < 4)
            def _():
                remote(wb.at[yy], wb.at[yy], ring_send.at[k], ring_recv.at[k], up).start()

        @pl.when((zz == 0) & (odd == 0) & (k > 0))
        def _():
            remote(wb.at[yy], wb.at[yy], ring_send.at[k + 3], ring_recv.at[k + 3], down).wait_recv()

            @pl.when(k < 3)
            def _():
                remote(wb.at[yy], wb.at[yy], ring_send.at[k + 4], ring_recv.at[k + 4], down).start()

        latents = jnp.concatenate(
            [chip_rows(zh + k)[:, :LATENT] for k in range(9)], axis=0
        )
        keys = jnp.dot(latents, wb[yy, zz, :LATENT, :], preferred_element_type=F32).astype(BF)
        values = jnp.dot(latents, wb[yy, zz, LATENT:, :], preferred_element_type=F32).astype(BF)
        kr[0, :, :NOPE] = keys[:, :NOPE]
        kr[1, :, :NOPE] = keys[:, NOPE:]
        pick = jnp.where(
            lax.broadcasted_iota(jnp.int32, (64, 384), 0)
            == 2 * pair + (lax.broadcasted_iota(jnp.int32, (64, 384), 1) >= 192).astype(jnp.int32),
            F32(1.0), F32(0.0),
        ).astype(BF)
        scaled = q2[j].astype(F32) * jnp.dot(pw[...], pick, preferred_element_type=F32)
        turned = pltpu.roll(scaled, 320, 1)
        queries = [
            jnp.concatenate(
                [scaled[:, :128], jnp.where(lane < ROPE, scaled[:, 128:256], noth[...])], axis=1
            ).astype(BF),
            jnp.concatenate(
                [turned[:, 128:256], jnp.where(lane < ROPE, turned[:, 256:], noth[...])], axis=1
            ).astype(BF),
        ]
        for h in range(2):
            scores = lax.dot_general(
                queries[h], kr[h], (((1,), (1,)), ((), ())), preferred_element_type=F32
            )
            scores = jnp.concatenate(
                [scores[:, : WINDOW - CHIP], scores[:, WINDOW - CHIP :] + causal[...]], axis=1
            )
            largest = jnp.max(scores, axis=1, keepdims=True)
            weights = jnp.exp2((scores - largest) * scale)
            sums = jnp.sum(weights, axis=1, keepdims=True)
            weighted = jnp.dot(
                weights.astype(BF), values[:, h * VDIM : (h + 1) * VDIM],
                preferred_element_type=F32,
            )
            obuf[j, :, h * VDIM : (h + 1) * VDIM] = (weighted / sums).astype(BF)
        columns = pl.ds(pl.multiple_of(pair * 256, 256), 256)
        out_ref[:, columns] = obuf[j, my_rows, :]
        remote(
            obuf.at[j, other_rows], out_ref.at[:, columns], out_send.at[j], out_recv.at[j], sibling
        ).start()
        return carry

    lax.fori_loop(0, 16, one_pair, 0)

    def finish(j, carry):
        columns = pl.ds(pl.multiple_of((2 * j + 1 - c) * 256, 256), 256)
        remote(
            obuf.at[j, other_rows], out_ref.at[:, columns], out_send.at[j], out_recv.at[j], sibling
        ).wait()
        return carry

    lax.fori_loop(0, 16, finish, 0)
    for step in steps:
        step.wait_send()
    last.wait_send()
    for k in range(7):
        remote(wb.at[y], wb.at[y], ring_send.at[k], ring_recv.at[k], up).wait_send()


def body(queries, exponents, latent, segments, key_weight, value_weight):
    documents = (segments[:, None] == jnp.arange(64, dtype=jnp.int32)[None, :]).astype(BF)
    wide = jnp.concatenate([latent, documents], axis=1)
    hbm = pl.BlockSpec(memory_space=pl.ANY)
    dma = pltpu.SemaphoreType.DMA
    return pl.pallas_call(
        kernel,
        out_shape=jax.ShapeDtypeStruct((ROWS, 8192), BF),
        in_specs=[hbm] * 5,
        out_specs=pl.BlockSpec(memory_space=pltpu.VMEM),
        scratch_shapes=[
            pltpu.VMEM((8, 2, 1024, 256), BF),
            pltpu.VMEM((16, CHIP, 384), BF),
            pltpu.VMEM((CHIP, 64), jnp.int32),
            pltpu.VMEM((5, 2, 2, ROWS, WIDE), BF),
            pltpu.VMEM((2, WINDOW, 256), BF),
            pltpu.VMEM((16, CHIP, 256), BF),
            pltpu.VMEM((CHIP, 64), BF),
            pltpu.VMEM((CHIP, CHIP), F32),
            pltpu.VMEM((CHIP, CHIP), F32),
            dma((5,)),
            dma((2,)), dma((2,)),
            dma((3,)), dma((3,)),
            dma((4,)), dma((4,)),
            dma((5,)), dma((5,)),
            dma((7,)), dma((7,)),
            dma((16,)), dma((16,)),
        ],
        compiler_params=pltpu.CompilerParams(
            collective_id=0, has_side_effects=True, vmem_limit_bytes=52 * 1024 * 1024
        ),
    )(queries, exponents, wide, key_weight, value_weight)


def solution(mesh):
    both = ("blk", "head")
    placed = (
        P(both, None), P(both, None), P(both, None), P(both), P(None, "head"), P(None, "head"),
    )
    return jax.shard_map(
        body, mesh=mesh, in_specs=placed, out_specs=P(both, None), check_vma=False
    )
```

```python
import math

import jax
import jax.numpy as jnp
from jax import lax
from jax.experimental import pallas as pl
from jax.experimental.pallas import tpu as pltpu
from jax.sharding import PartitionSpec as P

NOPE = 128
ROPE = 64
LATENT = 512
VDIM = 128
WIDE = 640
ROWS = 64
CHIP = 128
WINDOW = 1152
UNION = 1408
BIG = 1e30
SPLIT = 2
BF = jnp.bfloat16
F32 = jnp.float32


def kernel(
    q_ref, e_ref, lat_ref, seg_ref, kw_ref, vw_ref, out_ref,
    wn, wf, wcur, q2, ev, lat, own, seg, kr, obuf, pw, noth, causal,
    local_sem, q_send, q_recv, e_send, e_recv, lat_send, lat_recv, share_send, share_recv,
    quarter_send, quarter_recv, spread_send, spread_recv,
    az_send, az_recv, ax_send, ax_recv, bz_send, bz_recv, bx_send, bx_recv, out_send, out_recv,
):
    blk = lax.axis_index("blk")
    head = lax.axis_index("head")
    n_blk = lax.axis_size("blk")
    zl, x = blk // 4, blk % 4
    y, zh, c = head // 4, (head // 2) % 2, head % 2
    z = zh * 4 + zl
    a = y % 2
    mate = (y + 1 - 2 * a) % 8

    def remote(src, dst, send, recv, device):
        return pltpu.make_async_remote_copy(
            src_ref=src, dst_ref=dst, send_sem=send, recv_sem=recv, device_id=device
        )

    def at(b, yy, zz, cc):
        return {"blk": b, "head": yy * 4 + zz * 2 + cc}

    def along_x(d):
        return at(zl * 4 + (x + d) % 4, y, zh, c)

    def along_y(d):
        return at(blk, (y + d) % 8, zh, c)

    def along_z(d):
        other = (z + d) % 8
        return at(other % 4 * 4 + x, y, other // 4, c)

    def onward(d):
        return at((blk + n_blk + (y + d + 8) // 8 - 1) % n_blk, (y + d + 8) % 8, zh, c)

    team = [(a, 1 - c), (1 - a, c), (1 - a, 1 - c)]
    team_at = [at(blk, y, zh, 1 - c), at(blk, mate, zh, c), at(blk, mate, zh, 1 - c)]
    extra_at = at(
        (blk + jnp.where(a == 0, (y + 5) // 8, 0)) % n_blk,
        jnp.where(a == 0, (y + 5) % 8, mate), zh, c,
    )
    extra_from = at(
        (blk + n_blk - jnp.where(a == 0, 0, (12 - y) // 8)) % n_blk,
        jnp.where(a == 0, mate, (y + 3) % 8), zh, c,
    )

    def token_rows(aa, cc):
        return pl.ds(pl.multiple_of((aa * 2 + cc) * ROWS, ROWS), ROWS)

    my_rows = token_rows(a, c)

    lat_in = pltpu.make_async_copy(lat_ref, own, local_sem.at[0])
    lat_in.start()
    seg_in = pltpu.make_async_copy(seg_ref, seg, local_sem.at[5])
    seg_in.start()
    wk_in = pltpu.make_async_copy(kw_ref, wn.at[zh, pl.ds(0, 512)], local_sem.at[1])
    wk_in.start()
    wv_in = pltpu.make_async_copy(vw_ref, wn.at[zh, pl.ds(512, 512)], local_sem.at[2])
    wv_in.start()
    e_in = pltpu.make_async_copy(e_ref, ev.at[my_rows], local_sem.at[3])
    e_in.start()

    def pair_of(j, aa, cc):
        return ((2 * (j // 2) + aa) * 2 + j % 2) * 2 + cc

    def q_columns(pair):
        return pl.ds(pl.multiple_of(pair * 384, 384), 384)

    def q_keep(j, carry):
        pltpu.make_async_copy(
            q_ref.at[:, q_columns(pair_of(j, a, c))], q2.at[j, my_rows], local_sem.at[4]
        ).start()
        return carry

    lax.fori_loop(0, 8, q_keep, 0)

    barrier = pltpu.get_barrier_semaphore()
    others = team_at + [extra_at, extra_from, onward(1), onward(-1), onward(4), onward(-4)]
    others += [along_x(d) for d in (1, 2, 3)]
    others += [along_y(d) for d in (2, 4, 6)] + [along_z(d) for d in (1, 4, 7)]
    for other in others:
        pl.semaphore_signal(barrier, inc=1, device_id=other)

    lat_in.wait()
    seg_in.wait()
    ids = lax.broadcasted_iota(jnp.int32, (CHIP, CHIP), 0)
    numbers = jnp.concatenate([seg[...], seg[...]], axis=1)
    hot = jnp.where(jnp.broadcast_to(numbers, (CHIP, CHIP)) == ids, F32(1.0), F32(0.0))
    hot = hot.T[:ROWS, :ROWS].astype(BF)
    lat[4 + a, zh, c] = jnp.concatenate([own[...], hot], axis=1)
    pl.semaphore_wait(barrier, len(others))

    def lat_pair():
        part = lat.at[4 + a, zh, c]
        return remote(part, part, lat_send.at[5], lat_recv.at[5], along_z(4))

    def lat_step(k):
        return remote(
            lat.at[4 + a - k, :, c], lat.at[4 - a - k, :, c], lat_send.at[k], lat_recv.at[k],
            onward(1),
        )

    def lat_four():
        return remote(
            lat.at[4 + a, :, c], lat.at[a, :, c], lat_send.at[3], lat_recv.at[3], onward(4)
        )

    def lat_extra():
        return remote(
            lat.at[4 + a, :, c], lat.at[5 * a, :, c], lat_send.at[4], lat_recv.at[4], extra_at
        )

    def share(k):
        slot = 5 - 5 * a if k == 5 else 4 + a - k
        part = lat.at[slot, :, c]
        return remote(part, part, share_send.at[k], share_recv.at[k], team_at[0])

    def q_part(r, zz, i):
        j = (y // 2 + r) % 4 * 2 + zz
        return remote(
            q_ref.at[:, q_columns(pair_of(j, team[i][0], team[i][1]))], q2.at[j, my_rows],
            q_send.at[r * 3 + i], q_recv.at[r * 3 + i], team_at[i],
        )

    def q_both(r, i):
        part = q2.at[pl.ds((y // 2 + r) % 4 * 2, 2), my_rows]
        return remote(part, part, q_send.at[r * 3 + i], q_recv.at[r * 3 + i], team_at[i])

    def q_start(r):
        for i in range(3):
            for zz in range(2):
                q_part(r, zz, i).start()

    def e_part(i):
        return remote(e_ref, ev.at[my_rows], e_send.at[i], e_recv.at[i], team_at[i])

    def quarter(mine):
        part = wn.at[zh if mine else 1 - zh, pl.ds(pl.multiple_of(x * 256, 256), 256)]
        return part

    def quarter_pair():
        return remote(
            quarter(True), quarter(True), quarter_send.at[3], quarter_recv.at[3], along_z(4)
        )

    def quarter_on(d):
        return remote(
            quarter(False), quarter(False), quarter_send.at[d - 1], quarter_recv.at[d - 1],
            along_x(d),
        )

    piece = pl.ds(pl.multiple_of((zl * 4 + x) * 64, 64), 64)

    def spread(d):
        return remote(
            wn.at[zh, piece], wf.at[z, x, 3 - d // 2], spread_send.at[0], spread_recv.at[0],
            along_y(d),
        )

    def spread_all():
        part = wf.at[z, x]
        return remote(part, part, spread_send.at[0], spread_recv.at[0], along_y(2))

    def az(way, k):
        held = (z + (9 - k if way == 0 else 7 + k)) % 8
        part = wf.at[held, x, pl.ds(0, SPLIT)]
        i = way * 4 + k - 1
        return remote(part, part, az_send.at[i], az_recv.at[i], along_z(1 if way == 0 else 7))

    def ax(offset, d):
        part = wf.at[(z + offset) % 8, x, pl.ds(0, SPLIT)]
        return remote(part, part, ax_send.at[d - 1], ax_recv.at[d - 1], along_x(d))

    def ax_all(d):
        part = wf.at[:, x, pl.ds(0, SPLIT)]
        return remote(part, part, ax_send.at[d - 1], ax_recv.at[d - 1], along_x(d))

    def bx(d):
        part = wf.at[z, x, pl.ds(SPLIT, 3 - SPLIT)]
        return remote(part, part, bx_send.at[d - 1], bx_recv.at[d - 1], along_x(d))

    def bz(way, k):
        held = (z + (9 - k if way == 0 else 7 + k)) % 8
        part = wf.at[held, :, pl.ds(SPLIT, 3 - SPLIT)]
        i = way * 4 + k - 1
        return remote(part, part, bz_send.at[i], bz_recv.at[i], along_z(1 if way == 0 else 7))

    def ax_start(offset):
        for d in (1, 3, 2):
            ax(offset, d).start()

    def a_begin():
        spread_all().wait_recv()
        az(0, 1).start()
        az(1, 1).start()
        for d in (1, 3, 2):
            bx(d).start()
        ax_start(0)

    def b_begin():
        for d in (1, 3, 2):
            bx(d).wait_recv()
        bz(0, 1).start()
        bz(1, 1).start()

    def a_next(k):
        az(1, k).wait_recv()
        if k < 4:
            az(1, k + 1).start()
            az(0, k).wait_recv()
            if k < 3:
                az(0, k + 1).start()
            ax_start(8 - k)
        ax_start(k)

    def b_next(k):
        bz(0, k).wait_recv()
        if k < 4:
            bz(0, k + 1).start()
            bz(1, k).wait_recv()
            if k < 3:
                bz(1, k + 1).start()

    def lat_next(k):
        lat_step(k).wait_recv()
        if k < 2:
            lat_step(k + 1).start()
        share(k + 1).start()

    lat_pair().start()
    wk_in.wait()
    wv_in.wait()
    for d in (4, 2, 6):
        spread(d).start()
    quarter_pair().start()
    for i in range(3):
        e_part(i).start()
    q_start(0)

    lat_pair().wait_recv()
    lat_step(0).start()
    lat_extra().start()
    lat_four().start()
    share(0).start()
    quarter_pair().wait_recv()
    for d in (1, 3, 2):
        quarter_on(d).start()
    a_begin()
    lat_next(0)
    b_begin()
    lat_next(1)
    a_next(1)
    q_start(1)
    lat_next(2)
    lat_four().wait_recv()
    share(4).start()
    lat_extra().wait_recv()
    share(5).start()
    q_start(2)
    q_start(3)
    a_next(2)
    b_next(1)
    e_in.wait()
    for i in range(3):
        e_part(i).wait_recv()
    powers = jnp.zeros((4 * ROWS, 64), F32)
    for level in range(-4, 5):
        powers = powers + jnp.where(ev[...] == level, F32(2.0**level), F32(0.0))
    pw[...] = powers.astype(BF)
    causal[...] = jnp.where(
        lax.broadcasted_iota(jnp.int32, (CHIP, CHIP), 1)
        <= lax.broadcasted_iota(jnp.int32, (CHIP, CHIP), 0),
        F32(0.0), F32(-BIG),
    )
    pltpu.make_async_copy(q2.at[:, my_rows], q2.at[:, my_rows], local_sem.at[4]).wait()
    for d in (1, 3, 2):
        quarter_on(d).wait_recv()
    for k in range(6):
        share(k).wait_recv()

    def chip_rows(slot):
        block = lat[slot // 2, slot % 2]
        return block.reshape(CHIP, WIDE)

    tail = jnp.concatenate([chip_rows(zh + k)[:, LATENT:] for k in range(11)], axis=0)
    kr[0, :, NOPE:] = tail
    kr[1, :, NOPE:] = tail
    lane = lax.broadcasted_iota(jnp.int32, (2 * CHIP, CHIP), 1)
    own_tail = jnp.concatenate([chip_rows(zh + k)[:, LATENT:] for k in (8, 10)], axis=0)
    noth[...] = jnp.where(lane < ROPE, F32(0.0), (own_tail.astype(F32) - 1.0) * F32(BIG))
    scale = F32(math.log2(math.e) / math.sqrt(NOPE + ROPE))

    def q_ready(r):
        for i in range(3):
            q_both(r, i).wait_recv()

    def far_a():
        for d in (1, 3, 2):
            ax_all(d).wait_recv()

    events = {
        0: [lambda: q_ready(0), lambda: a_next(3), lambda: b_next(2)],
        1: [lambda: a_next(4), lambda: b_next(3)],
        2: [lambda: q_ready(1), far_a],
        3: [lambda: b_next(4)],
        4: [lambda: q_ready(2)],
        6: [lambda: q_ready(3)],
    }

    def nt(left, right):
        return lax.dot_general(
            left, right, (((1,), (1,)), ((), ())), preferred_element_type=F32
        )

    def one_pair(t, carry):
        for when, todo in events.items():
            for event in todo:
                pl.when(t == when)(event)

        r = t // 2
        zz = (zh + t) % 2
        j = (y // 2 + r) % 4 * 2 + zz
        pair = pair_of(j, a, c)

        @pl.when(r > 0)
        def _():
            wcur[...] = wf[pl.ds(zz * 4, 4), :, jnp.maximum(r - 1, 0)].reshape(1024, 256)

        @pl.when(r == 0)
        def _():
            wcur[...] = wn[zz]

        latents = jnp.concatenate([chip_rows(zh + k)[:, :LATENT] for k in range(11)], axis=0)
        keys = jnp.dot(latents, wcur[:LATENT, :], preferred_element_type=F32).astype(BF)
        values = jnp.dot(latents, wcur[LATENT:, :], preferred_element_type=F32).astype(BF)
        kr[0, :, :NOPE] = keys[:, :NOPE]
        kr[1, :, :NOPE] = keys[:, NOPE:]
        pick = jnp.where(
            lax.broadcasted_iota(jnp.int32, (64, 384), 0)
            == 2 * pair + (lax.broadcasted_iota(jnp.int32, (64, 384), 1) >= 192).astype(jnp.int32),
            F32(1.0), F32(0.0),
        ).astype(BF)
        scaled = q2[j].astype(F32) * jnp.dot(pw[...], pick, preferred_element_type=F32)
        turned = pltpu.roll(scaled, 320, 1)
        queries = [
            jnp.concatenate(
                [scaled[:, :128], jnp.where(lane < ROPE, scaled[:, 128:256], noth[...])], axis=1
            ).astype(BF),
            jnp.concatenate(
                [turned[:, 128:256], jnp.where(lane < ROPE, turned[:, 256:], noth[...])], axis=1
            ).astype(BF),
        ]
        for h in range(2):
            both = nt(queries[h], kr[h, 256:WINDOW])
            first = nt(queries[h][:CHIP], kr[h, :256])
            last = nt(queries[h][CHIP:], kr[h, WINDOW:])
            scores = jnp.concatenate(
                [
                    jnp.concatenate([first, both[:CHIP]], axis=1),
                    jnp.concatenate([both[CHIP:], last], axis=1),
                ],
                axis=0,
            )
            mask = jnp.concatenate([causal[...], causal[...]], axis=0)
            scores = jnp.concatenate(
                [scores[:, : WINDOW - CHIP], scores[:, WINDOW - CHIP :] + mask], axis=1
            )
            largest = jnp.max(scores, axis=1, keepdims=True)
            weights = jnp.exp2((scores - largest) * scale)
            sums = jnp.sum(weights, axis=1, keepdims=True)
            weights = weights.astype(BF)
            for b in range(2):
                rows = slice(b * CHIP, (b + 1) * CHIP)
                weighted = jnp.dot(
                    weights[rows],
                    values[b * 256 : b * 256 + WINDOW, h * VDIM : (h + 1) * VDIM],
                    preferred_element_type=F32,
                )
                obuf[j, rows, h * VDIM : (h + 1) * VDIM] = (weighted / sums[rows]).astype(BF)
        columns = pl.ds(pl.multiple_of(pair * 256, 256), 256)
        for i in range(3):
            out_part(j, i, columns).start()
        out_ref[:, columns] = obuf[j, my_rows, :]
        return carry

    def out_part(j, i, columns):
        return remote(
            obuf.at[j, token_rows(team[i][0], team[i][1])], out_ref.at[:, columns],
            out_send.at[i * 8 + j], out_recv.at[i * 8 + j], team_at[i],
        )

    lax.fori_loop(0, 8, one_pair, 0)

    def finish(j, carry):
        for i in range(3):
            pair = pair_of(j, team[i][0], team[i][1])
            out_part(j, i, pl.ds(pl.multiple_of(pair * 256, 256), 256)).wait()
        return carry

    lax.fori_loop(0, 8, finish, 0)
    for i in range(3):
        e_part(i).wait_send()
        for r in range(4):
            q_both(r, i).wait_send()
    lat_pair().wait_send()
    lat_four().wait_send()
    lat_extra().wait_send()
    for k in range(3):
        lat_step(k).wait_send()
    for k in range(6):
        share(k).wait_send()
    quarter_pair().wait_send()
    spread_all().wait_send()
    for d in (1, 2, 3):
        quarter_on(d).wait_send()
        ax_all(d).wait_send()
        bx(d).wait_send()
    for k in range(1, 5):
        az(1, k).wait_send()
        bz(0, k).wait_send()
        if k < 4:
            az(0, k).wait_send()
            bz(1, k).wait_send()


def body(queries, exponents, latent, segments, key_weight, value_weight):
    documents = segments.reshape(1, ROWS)
    hbm = pl.BlockSpec(memory_space=pl.ANY)
    dma = pltpu.SemaphoreType.DMA
    return pl.pallas_call(
        kernel,
        out_shape=jax.ShapeDtypeStruct((ROWS, 8192), BF),
        in_specs=[hbm] * 6,
        out_specs=pl.BlockSpec(memory_space=pltpu.VMEM),
        scratch_shapes=[
            pltpu.VMEM((2, 1024, 256), BF),
            pltpu.VMEM((8, 4, 3, 64, 256), BF),
            pltpu.VMEM((1024, 256), BF),
            pltpu.VMEM((8, 4 * ROWS, 384), BF),
            pltpu.VMEM((4 * ROWS, 64), jnp.int32),
            pltpu.VMEM((6, 2, 2, ROWS, WIDE), BF),
            pltpu.VMEM((ROWS, 576), BF),
            pltpu.VMEM((1, ROWS), jnp.int32),
            pltpu.VMEM((2, UNION, 256), BF),
            pltpu.VMEM((8, 4 * ROWS, 256), BF),
            pltpu.VMEM((4 * ROWS, 64), BF),
            pltpu.VMEM((2 * CHIP, CHIP), F32),
            pltpu.VMEM((CHIP, CHIP), F32),
            dma((6,)),
            dma((12,)), dma((12,)),
            dma((3,)), dma((3,)),
            dma((6,)), dma((6,)),
            dma((6,)), dma((6,)),
            dma((4,)), dma((4,)),
            dma((1,)), dma((1,)),
            dma((8,)), dma((8,)),
            dma((3,)), dma((3,)),
            dma((8,)), dma((8,)),
            dma((3,)), dma((3,)),
            dma((24,)), dma((24,)),
        ],
        compiler_params=pltpu.CompilerParams(
            collective_id=0, has_side_effects=True, vmem_limit_bytes=58 * 1024 * 1024
        ),
    )(queries, exponents, latent, documents, key_weight, value_weight)


def solution(mesh):
    both = ("blk", "head")
    placed = (
        P(both, None), P(both, None), P(both, None), P(both), P(None, "head"), P(None, "head"),
    )
    return jax.shard_map(
        body, mesh=mesh, in_specs=placed, out_specs=P(both, None), check_vma=False
    )
```

```python
import math

import jax
import jax.numpy as jnp
from jax import lax
from jax.experimental import pallas as pl
from jax.experimental.pallas import tpu as pltpu
from jax.sharding import PartitionSpec as P

NOPE = 128
ROPE = 64
LATENT = 512
VDIM = 128
WIDE = 640
ROWS = 64
CHIP = 128
WINDOW = 1152
UNION = 1408
BIG = 1e30
SPLIT = 112
BF = jnp.bfloat16
F32 = jnp.float32


def kernel(
    q_ref, e_ref, lat_ref, seg_ref, kw_ref, vw_ref, out_ref,
    wn, wf, wcur, q2, ev, lat, own, seg, kr, obuf, pw, noth, causal,
    local_sem, q_send, q_recv, e_send, e_recv, lat_send, lat_recv, share_send, share_recv,
    quarter_send, quarter_recv, spread_send, spread_recv,
    az_send, az_recv, ax_send, ax_recv, bz_send, bz_recv, bx_send, bx_recv, out_send, out_recv,
):
    blk = lax.axis_index("blk")
    head = lax.axis_index("head")
    n_blk = lax.axis_size("blk")
    zl, x = blk // 4, blk % 4
    y, zh, c = head // 4, (head // 2) % 2, head % 2
    z = zh * 4 + zl
    a = y % 2
    mate = (y + 1 - 2 * a) % 8

    def remote(src, dst, send, recv, device):
        return pltpu.make_async_remote_copy(
            src_ref=src, dst_ref=dst, send_sem=send, recv_sem=recv, device_id=device
        )

    def at(b, yy, zz, cc):
        return {"blk": b, "head": yy * 4 + zz * 2 + cc}

    def along_x(d):
        return at(zl * 4 + (x + d) % 4, y, zh, c)

    def along_y(d):
        return at(blk, (y + d) % 8, zh, c)

    def along_z(d):
        other = (z + d) % 8
        return at(other % 4 * 4 + x, y, other // 4, c)

    def onward(d):
        return at((blk + n_blk + (y + d + 8) // 8 - 1) % n_blk, (y + d + 8) % 8, zh, c)

    team = [(a, 1 - c), (1 - a, c), (1 - a, 1 - c)]
    team_at = [at(blk, y, zh, 1 - c), at(blk, mate, zh, c), at(blk, mate, zh, 1 - c)]
    extra_at = at(
        (blk + jnp.where(a == 0, (y + 5) // 8, 0)) % n_blk,
        jnp.where(a == 0, (y + 5) % 8, mate), zh, c,
    )
    extra_from = at(
        (blk + n_blk - jnp.where(a == 0, 0, (12 - y) // 8)) % n_blk,
        jnp.where(a == 0, mate, (y + 3) % 8), zh, c,
    )

    def token_rows(aa, cc):
        return pl.ds(pl.multiple_of((aa * 2 + cc) * ROWS, ROWS), ROWS)

    my_rows = token_rows(a, c)

    lat_in = pltpu.make_async_copy(lat_ref, own, local_sem.at[0])
    lat_in.start()
    seg_in = pltpu.make_async_copy(seg_ref, seg, local_sem.at[5])
    seg_in.start()
    wk_in = pltpu.make_async_copy(kw_ref, wn.at[zh, pl.ds(0, 512)], local_sem.at[1])
    wk_in.start()
    wv_in = pltpu.make_async_copy(vw_ref, wn.at[zh, pl.ds(512, 512)], local_sem.at[2])
    wv_in.start()
    e_in = pltpu.make_async_copy(e_ref, ev.at[my_rows], local_sem.at[3])
    e_in.start()

    def pair_of(j, aa, cc):
        return ((2 * (j // 2) + aa) * 2 + j % 2) * 2 + cc

    def q_columns(pair):
        return pl.ds(pl.multiple_of(pair * 384, 384), 384)

    def q_keep(j, carry):
        pltpu.make_async_copy(
            q_ref.at[:, q_columns(pair_of(j, a, c))], q2.at[j, my_rows], local_sem.at[4]
        ).start()
        return carry

    lax.fori_loop(0, 8, q_keep, 0)

    barrier = pltpu.get_barrier_semaphore()
    others = team_at + [extra_at, extra_from, onward(1), onward(-1)]
    others += [along_x(d) for d in (1, 2, 3)]
    others += [along_y(d) for d in (2, 4, 6)] + [along_z(d) for d in (1, 4, 7)]
    for other in others:
        pl.semaphore_signal(barrier, inc=1, device_id=other)

    lat_in.wait()
    seg_in.wait()
    ids = lax.broadcasted_iota(jnp.int32, (CHIP, CHIP), 0)
    numbers = jnp.concatenate([seg[...], seg[...]], axis=1)
    hot = jnp.where(jnp.broadcast_to(numbers, (CHIP, CHIP)) == ids, F32(1.0), F32(0.0))
    hot = hot.T[:ROWS, :ROWS].astype(BF)
    lat[4 + a, zh, c] = jnp.concatenate([own[...], hot], axis=1)
    pl.semaphore_wait(barrier, len(others))

    def lat_pair():
        part = lat.at[4 + a, zh, c]
        return remote(part, part, lat_send.at[5], lat_recv.at[5], along_z(4))

    def lat_step(k):
        return remote(
            lat.at[4 + a - k, :, c], lat.at[4 - a - k, :, c], lat_send.at[k], lat_recv.at[k],
            onward(1),
        )

    def lat_second():
        return remote(
            lat.at[5 - 5 * a, :, c], lat.at[1 - a, :, c], lat_send.at[3], lat_recv.at[3], extra_at
        )

    def lat_extra():
        return remote(
            lat.at[4 + a, :, c], lat.at[5 * a, :, c], lat_send.at[4], lat_recv.at[4], extra_at
        )

    def share(k):
        slot = 5 - 5 * a if k == 5 else 4 + a - k
        part = lat.at[slot, :, c]
        return remote(part, part, share_send.at[k], share_recv.at[k], team_at[0])

    def q_part(r, zz, i):
        j = (y // 2 + r) % 4 * 2 + zz
        return remote(
            q_ref.at[:, q_columns(pair_of(j, team[i][0], team[i][1]))], q2.at[j, my_rows],
            q_send.at[r * 3 + i], q_recv.at[r * 3 + i], team_at[i],
        )

    def q_both(r, i):
        part = q2.at[pl.ds((y // 2 + r) % 4 * 2, 2), my_rows]
        return remote(part, part, q_send.at[r * 3 + i], q_recv.at[r * 3 + i], team_at[i])

    def q_start(r):
        for i in range(3):
            for zz in range(2):
                q_part(r, zz, i).start()

    def e_part(i):
        return remote(e_ref, ev.at[my_rows], e_send.at[i], e_recv.at[i], team_at[i])

    def quarter(mine):
        part = wn.at[zh if mine else 1 - zh, pl.ds(pl.multiple_of(x * 256, 256), 256)]
        return part

    def quarter_pair():
        return remote(
            quarter(True), quarter(True), quarter_send.at[3], quarter_recv.at[3], along_z(4)
        )

    def quarter_on(d):
        return remote(
            quarter(False), quarter(False), quarter_send.at[d - 1], quarter_recv.at[d - 1],
            along_x(d),
        )

    piece = pl.ds(pl.multiple_of((zl * 4 + x) * 64, 64), 64)

    def spread(d):
        return remote(
            wn.at[zh, piece], wf.at[z, x, pl.ds((3 - d // 2) * 64, 64)], spread_send.at[0], spread_recv.at[0],
            along_y(d),
        )

    def spread_all():
        part = wf.at[z, x]
        return remote(part, part, spread_send.at[0], spread_recv.at[0], along_y(2))

    def az(way, k):
        held = (z + (9 - k if way == 0 else 7 + k)) % 8
        part = wf.at[held, x, pl.ds(0, SPLIT)]
        i = way * 4 + k - 1
        return remote(part, part, az_send.at[i], az_recv.at[i], along_z(1 if way == 0 else 7))

    def ax(offset, d):
        part = wf.at[(z + offset) % 8, x, pl.ds(0, SPLIT)]
        return remote(part, part, ax_send.at[d - 1], ax_recv.at[d - 1], along_x(d))

    def ax_all(d):
        part = wf.at[:, x, pl.ds(0, SPLIT)]
        return remote(part, part, ax_send.at[d - 1], ax_recv.at[d - 1], along_x(d))

    def bx(d):
        part = wf.at[z, x, pl.ds(SPLIT, 192 - SPLIT)]
        return remote(part, part, bx_send.at[d - 1], bx_recv.at[d - 1], along_x(d))

    def bz(way, k):
        held = (z + (9 - k if way == 0 else 7 + k)) % 8
        part = wf.at[held, :, pl.ds(SPLIT, 192 - SPLIT)]
        i = way * 4 + k - 1
        return remote(part, part, bz_send.at[i], bz_recv.at[i], along_z(1 if way == 0 else 7))

    def ax_start(offset):
        for d in (1, 3, 2):
            ax(offset, d).start()

    def a_begin():
        spread_all().wait_recv()
        az(0, 1).start()
        az(1, 1).start()
        for d in (1, 3, 2):
            bx(d).start()
        ax_start(0)

    def b_begin():
        for d in (1, 3, 2):
            bx(d).wait_recv()
        bz(0, 1).start()
        bz(1, 1).start()

    def a_next(k):
        az(1, k).wait_recv()
        if k < 4:
            az(1, k + 1).start()
            az(0, k).wait_recv()
            if k < 3:
                az(0, k + 1).start()
            ax_start(8 - k)
        ax_start(k)

    def b_next(k):
        bz(0, k).wait_recv()
        if k < 4:
            bz(0, k + 1).start()
            bz(1, k).wait_recv()
            if k < 3:
                bz(1, k + 1).start()

    def lat_next(k):
        lat_step(k).wait_recv()
        if k < 2:
            lat_step(k + 1).start()
        share(k + 1).start()

    lat_pair().start()
    wk_in.wait()
    wv_in.wait()
    for d in (4, 2, 6):
        spread(d).start()
    lat_pair().wait_recv()
    lat_step(0).start()
    lat_extra().start()
    share(0).start()
    a_begin()
    for i in range(3):
        e_part(i).start()
    lat_next(0)
    a_next(1)
    b_begin()
    lat_extra().wait_recv()
    lat_second().start()
    share(5).start()
    a_next(2)
    lat_next(1)
    q_start(0)
    b_next(1)
    a_next(3)
    lat_next(2)
    a_next(4)
    lat_second().wait_recv()
    share(4).start()
    q_start(1)
    b_next(2)
    quarter_pair().start()
    q_start(2)
    q_start(3)
    e_in.wait()
    for i in range(3):
        e_part(i).wait_recv()
    powers = jnp.zeros((4 * ROWS, 64), F32)
    for level in range(-4, 5):
        powers = powers + jnp.where(ev[...] == level, F32(2.0**level), F32(0.0))
    pw[...] = powers.astype(BF)
    causal[...] = jnp.where(
        lax.broadcasted_iota(jnp.int32, (CHIP, CHIP), 1)
        <= lax.broadcasted_iota(jnp.int32, (CHIP, CHIP), 0),
        F32(0.0), F32(-BIG),
    )
    pltpu.make_async_copy(q2.at[:, my_rows], q2.at[:, my_rows], local_sem.at[4]).wait()
    for k in range(6):
        share(k).wait_recv()

    def chip_rows(slot):
        block = lat[slot // 2, slot % 2]
        return block.reshape(CHIP, WIDE)

    tail = jnp.concatenate([chip_rows(zh + k)[:, LATENT:] for k in range(11)], axis=0)
    kr[0, :, NOPE:] = tail
    kr[1, :, NOPE:] = tail
    lane = lax.broadcasted_iota(jnp.int32, (2 * CHIP, CHIP), 1)
    own_tail = jnp.concatenate([chip_rows(zh + k)[:, LATENT:] for k in (8, 10)], axis=0)
    noth[...] = jnp.where(lane < ROPE, F32(0.0), (own_tail.astype(F32) - 1.0) * F32(BIG))
    scale = F32(math.log2(math.e) / math.sqrt(NOPE + ROPE))

    def q_ready(r):
        for i in range(3):
            q_both(r, i).wait_recv()

    def far_a():
        for d in (1, 3, 2):
            ax_all(d).wait_recv()

    def quarter_next():
        quarter_pair().wait_recv()
        for d in (1, 3, 2):
            quarter_on(d).start()

    def quarter_done():
        for d in (1, 3, 2):
            quarter_on(d).wait_recv()

    events = {
        0: [lambda: q_ready(0), lambda: b_next(3)],
        1: [quarter_next, lambda: q_ready(1), far_a],
        3: [lambda: q_ready(2), lambda: b_next(4)],
        5: [lambda: q_ready(3)],
        7: [quarter_done],
    }

    def nt(left, right):
        return lax.dot_general(
            left, right, (((1,), (1,)), ((), ())), preferred_element_type=F32
        )

    def one_pair(t, carry):
        for when, todo in events.items():
            for event in todo:
                pl.when(t == when)(event)

        r = (t + 1) // 2 % 4
        zz = (zh + t) % 2
        j = (y // 2 + r) % 4 * 2 + zz
        pair = pair_of(j, a, c)

        @pl.when(r > 0)
        def _():
            start = pl.multiple_of(jnp.maximum(r - 1, 0) * 64, 64)
            wcur[...] = wf[pl.ds(zz * 4, 4), :, pl.ds(start, 64)].reshape(1024, 256)

        @pl.when(r == 0)
        def _():
            wcur[...] = wn[zz]

        latents = jnp.concatenate([chip_rows(zh + k)[:, :LATENT] for k in range(11)], axis=0)
        keys = jnp.dot(latents, wcur[:LATENT, :], preferred_element_type=F32).astype(BF)
        values = jnp.dot(latents, wcur[LATENT:, :], preferred_element_type=F32).astype(BF)
        kr[0, :, :NOPE] = keys[:, :NOPE]
        kr[1, :, :NOPE] = keys[:, NOPE:]
        pick = jnp.where(
            lax.broadcasted_iota(jnp.int32, (64, 384), 0)
            == 2 * pair + (lax.broadcasted_iota(jnp.int32, (64, 384), 1) >= 192).astype(jnp.int32),
            F32(1.0), F32(0.0),
        ).astype(BF)
        scaled = q2[j].astype(F32) * jnp.dot(pw[...], pick, preferred_element_type=F32)
        turned = pltpu.roll(scaled, 320, 1)
        queries = [
            jnp.concatenate(
                [scaled[:, :128], jnp.where(lane < ROPE, scaled[:, 128:256], noth[...])], axis=1
            ).astype(BF),
            jnp.concatenate(
                [turned[:, 128:256], jnp.where(lane < ROPE, turned[:, 256:], noth[...])], axis=1
            ).astype(BF),
        ]
        for h in range(2):
            both = nt(queries[h], kr[h, 256:WINDOW])
            first = nt(queries[h][:CHIP], kr[h, :256])
            last = nt(queries[h][CHIP:], kr[h, WINDOW:])
            scores = jnp.concatenate(
                [
                    jnp.concatenate([first, both[:CHIP]], axis=1),
                    jnp.concatenate([both[CHIP:], last], axis=1),
                ],
                axis=0,
            )
            mask = jnp.concatenate([causal[...], causal[...]], axis=0)
            scores = jnp.concatenate(
                [scores[:, : WINDOW - CHIP], scores[:, WINDOW - CHIP :] + mask], axis=1
            )
            largest = jnp.max(scores, axis=1, keepdims=True)
            weights = jnp.exp2((scores - largest) * scale)
            sums = jnp.sum(weights, axis=1, keepdims=True)
            weights = weights.astype(BF)
            for b in range(2):
                rows = slice(b * CHIP, (b + 1) * CHIP)
                weighted = jnp.dot(
                    weights[rows],
                    values[b * 256 : b * 256 + WINDOW, h * VDIM : (h + 1) * VDIM],
                    preferred_element_type=F32,
                )
                obuf[j, rows, h * VDIM : (h + 1) * VDIM] = (weighted / sums[rows]).astype(BF)
        columns = pl.ds(pl.multiple_of(pair * 256, 256), 256)
        for i in range(3):
            out_part(j, i, columns).start()
        out_ref[:, columns] = obuf[j, my_rows, :]
        return carry

    def out_part(j, i, columns):
        return remote(
            obuf.at[j, token_rows(team[i][0], team[i][1])], out_ref.at[:, columns],
            out_send.at[i * 8 + j], out_recv.at[i * 8 + j], team_at[i],
        )

    lax.fori_loop(0, 8, one_pair, 0)

    def finish(j, carry):
        for i in range(3):
            pair = pair_of(j, team[i][0], team[i][1])
            out_part(j, i, pl.ds(pl.multiple_of(pair * 256, 256), 256)).wait()
        return carry

    lax.fori_loop(0, 8, finish, 0)
    for i in range(3):
        e_part(i).wait_send()
        for r in range(4):
            q_both(r, i).wait_send()
    lat_pair().wait_send()
    lat_second().wait_send()
    lat_extra().wait_send()
    for k in range(3):
        lat_step(k).wait_send()
    for k in range(6):
        share(k).wait_send()
    quarter_pair().wait_send()
    spread_all().wait_send()
    for d in (1, 2, 3):
        quarter_on(d).wait_send()
        ax_all(d).wait_send()
        bx(d).wait_send()
    for k in range(1, 5):
        az(1, k).wait_send()
        bz(0, k).wait_send()
        if k < 4:
            az(0, k).wait_send()
            bz(1, k).wait_send()


def body(queries, exponents, latent, segments, key_weight, value_weight):
    documents = segments.reshape(1, ROWS)
    hbm = pl.BlockSpec(memory_space=pl.ANY)
    dma = pltpu.SemaphoreType.DMA
    return pl.pallas_call(
        kernel,
        out_shape=jax.ShapeDtypeStruct((ROWS, 8192), BF),
        in_specs=[hbm] * 6,
        out_specs=pl.BlockSpec(memory_space=pltpu.VMEM),
        scratch_shapes=[
            pltpu.VMEM((2, 1024, 256), BF),
            pltpu.VMEM((8, 4, 192, 256), BF),
            pltpu.VMEM((1024, 256), BF),
            pltpu.VMEM((8, 4 * ROWS, 384), BF),
            pltpu.VMEM((4 * ROWS, 64), jnp.int32),
            pltpu.VMEM((6, 2, 2, ROWS, WIDE), BF),
            pltpu.VMEM((ROWS, 576), BF),
            pltpu.VMEM((1, ROWS), jnp.int32),
            pltpu.VMEM((2, UNION, 256), BF),
            pltpu.VMEM((8, 4 * ROWS, 256), BF),
            pltpu.VMEM((4 * ROWS, 64), BF),
            pltpu.VMEM((2 * CHIP, CHIP), F32),
            pltpu.VMEM((CHIP, CHIP), F32),
            dma((6,)),
            dma((12,)), dma((12,)),
            dma((3,)), dma((3,)),
            dma((6,)), dma((6,)),
            dma((6,)), dma((6,)),
            dma((4,)), dma((4,)),
            dma((1,)), dma((1,)),
            dma((8,)), dma((8,)),
            dma((3,)), dma((3,)),
            dma((8,)), dma((8,)),
            dma((3,)), dma((3,)),
            dma((24,)), dma((24,)),
        ],
        compiler_params=pltpu.CompilerParams(
            collective_id=0, has_side_effects=True, vmem_limit_bytes=58 * 1024 * 1024
        ),
    )(queries, exponents, latent, documents, key_weight, value_weight)


def solution(mesh):
    both = ("blk", "head")
    placed = (
        P(both, None), P(both, None), P(both, None), P(both), P(None, "head"), P(None, "head"),
    )
    return jax.shard_map(
        body, mesh=mesh, in_specs=placed, out_specs=P(both, None), check_vma=False
    )
```

```python
import math

import jax
import jax.numpy as jnp
from jax import lax
from jax.experimental import pallas as pl
from jax.experimental.pallas import tpu as pltpu
from jax.sharding import PartitionSpec as P

NOPE = 128
ROPE = 64
LATENT = 512
VDIM = 128
WIDE = 640
ROWS = 64
CHIP = 128
WINDOW = 1152
UNION = 1408
BIG = 1e30
SPLIT = 128
BF = jnp.bfloat16
F32 = jnp.float32


def kernel(
    q_ref, e_ref, lat_ref, seg_ref, kw_ref, vw_ref, out_ref,
    wn, wf, wcur, q2, ev, lat, own, seg, kr, obuf, pw, noth, causal,
    local_sem, q_send, q_recv, e_send, e_recv, lat_send, lat_recv, share_send, share_recv,
    quarter_send, quarter_recv, spread_send, spread_recv,
    az_send, az_recv, ax_send, ax_recv, bz_send, bz_recv, bx_send, bx_recv, out_send, out_recv,
):
    blk = lax.axis_index("blk")
    head = lax.axis_index("head")
    n_blk = lax.axis_size("blk")
    zl, x = blk // 4, blk % 4
    y, zh, c = head // 4, (head // 2) % 2, head % 2
    z = zh * 4 + zl
    a = y % 2
    mate = (y + 1 - 2 * a) % 8

    def remote(src, dst, send, recv, device):
        return pltpu.make_async_remote_copy(
            src_ref=src, dst_ref=dst, send_sem=send, recv_sem=recv, device_id=device
        )

    def at(b, yy, zz, cc):
        return {"blk": b, "head": yy * 4 + zz * 2 + cc}

    def along_x(d):
        return at(zl * 4 + (x + d) % 4, y, zh, c)

    def along_y(d):
        return at(blk, (y + d) % 8, zh, c)

    def along_z(d):
        other = (z + d) % 8
        return at(other % 4 * 4 + x, y, other // 4, c)

    def onward(d):
        return at((blk + n_blk + (y + d + 8) // 8 - 1) % n_blk, (y + d + 8) % 8, zh, c)

    team = [(a, 1 - c), (1 - a, c), (1 - a, 1 - c)]
    team_at = [at(blk, y, zh, 1 - c), at(blk, mate, zh, c), at(blk, mate, zh, 1 - c)]
    extra_at = at(
        (blk + jnp.where(a == 0, (y + 5) // 8, 0)) % n_blk,
        jnp.where(a == 0, (y + 5) % 8, mate), zh, c,
    )
    extra_from = at(
        (blk + n_blk - jnp.where(a == 0, 0, (12 - y) // 8)) % n_blk,
        jnp.where(a == 0, mate, (y + 3) % 8), zh, c,
    )

    def token_rows(aa, cc):
        return pl.ds(pl.multiple_of((aa * 2 + cc) * ROWS, ROWS), ROWS)

    my_rows = token_rows(a, c)

    lat_in = pltpu.make_async_copy(lat_ref, own, local_sem.at[0])
    lat_in.start()
    seg_in = pltpu.make_async_copy(seg_ref, seg, local_sem.at[5])
    seg_in.start()
    wk_in = pltpu.make_async_copy(kw_ref, wn.at[zh, pl.ds(0, 512)], local_sem.at[1])
    wk_in.start()
    wv_in = pltpu.make_async_copy(vw_ref, wn.at[zh, pl.ds(512, 512)], local_sem.at[2])
    wv_in.start()
    e_in = pltpu.make_async_copy(e_ref, ev.at[my_rows], local_sem.at[3])
    e_in.start()

    def pair_of(j, aa, cc):
        return ((2 * (j // 2) + aa) * 2 + j % 2) * 2 + cc

    def q_columns(pair):
        return pl.ds(pl.multiple_of(pair * 384, 384), 384)

    def q_keep(j, carry):
        pltpu.make_async_copy(
            q_ref.at[:, q_columns(pair_of(j, a, c))], q2.at[j, my_rows], local_sem.at[4]
        ).start()
        return carry

    lax.fori_loop(0, 8, q_keep, 0)

    barrier = pltpu.get_barrier_semaphore()
    others = team_at + [extra_at, extra_from, onward(1), onward(-1)]
    others += [along_x(d) for d in (1, 2, 3)]
    others += [along_y(d) for d in (2, 4, 6)] + [along_z(d) for d in (1, 4, 7)]
    for other in others:
        pl.semaphore_signal(barrier, inc=1, device_id=other)

    lat_in.wait()
    seg_in.wait()
    ids = lax.broadcasted_iota(jnp.int32, (CHIP, CHIP), 0)
    numbers = jnp.concatenate([seg[...], seg[...]], axis=1)
    hot = jnp.where(jnp.broadcast_to(numbers, (CHIP, CHIP)) == ids, F32(1.0), F32(0.0))
    hot = hot.T[:ROWS, :ROWS].astype(BF)
    lat[4 + a, zh, c] = jnp.concatenate([own[...], hot], axis=1)
    pl.semaphore_wait(barrier, len(others))

    def lat_pair():
        part = lat.at[4 + a, zh, c]
        return remote(part, part, lat_send.at[5], lat_recv.at[5], along_z(4))

    def lat_step(k):
        return remote(
            lat.at[4 + a - k, :, c], lat.at[4 - a - k, :, c], lat_send.at[k], lat_recv.at[k],
            onward(1),
        )

    def lat_second():
        return remote(
            lat.at[5 - 5 * a, :, c], lat.at[1 - a, :, c], lat_send.at[3], lat_recv.at[3], extra_at
        )

    def lat_extra():
        return remote(
            lat.at[4 + a, :, c], lat.at[5 * a, :, c], lat_send.at[4], lat_recv.at[4], extra_at
        )

    def share(k):
        slot = 5 - 5 * a if k == 5 else 4 + a - k
        part = lat.at[slot, :, c]
        return remote(part, part, share_send.at[k], share_recv.at[k], team_at[0])

    def q_part(r, zz, i):
        j = (y // 2 + r) % 4 * 2 + zz
        return remote(
            q_ref.at[:, q_columns(pair_of(j, team[i][0], team[i][1]))], q2.at[j, my_rows],
            q_send.at[r * 3 + i], q_recv.at[r * 3 + i], team_at[i],
        )

    def q_both(r, i):
        part = q2.at[pl.ds((y // 2 + r) % 4 * 2, 2), my_rows]
        return remote(part, part, q_send.at[r * 3 + i], q_recv.at[r * 3 + i], team_at[i])

    def q_start(r):
        for i in range(3):
            for zz in range(2):
                q_part(r, zz, i).start()

    def e_part(i):
        return remote(e_ref, ev.at[my_rows], e_send.at[i], e_recv.at[i], team_at[i])

    def quarter(mine):
        part = wn.at[zh if mine else 1 - zh, pl.ds(pl.multiple_of(x * 256, 256), 256)]
        return part

    def quarter_pair():
        return remote(
            quarter(True), quarter(True), quarter_send.at[3], quarter_recv.at[3], along_z(4)
        )

    def quarter_on(d):
        return remote(
            quarter(False), quarter(False), quarter_send.at[d - 1], quarter_recv.at[d - 1],
            along_x(d),
        )

    piece = pl.ds(pl.multiple_of((zl * 4 + x) * 64, 64), 64)

    def spread(d):
        return remote(
            wn.at[zh, piece], wf.at[z, x, pl.ds((3 - d // 2) * 64, 64)], spread_send.at[0], spread_recv.at[0],
            along_y(d),
        )

    def spread_all():
        part = wf.at[z, x]
        return remote(part, part, spread_send.at[0], spread_recv.at[0], along_y(2))

    def az(way, k):
        held = (z + (9 - k if way == 0 else 7 + k)) % 8
        part = wf.at[held, x, pl.ds(0, SPLIT)]
        i = way * 4 + k - 1
        return remote(part, part, az_send.at[i], az_recv.at[i], along_z(1 if way == 0 else 7))

    def ax(offset, d):
        part = wf.at[(z + offset) % 8, x, pl.ds(0, SPLIT)]
        return remote(part, part, ax_send.at[d - 1], ax_recv.at[d - 1], along_x(d))

    def ax_all(d):
        part = wf.at[:, x, pl.ds(0, SPLIT)]
        return remote(part, part, ax_send.at[d - 1], ax_recv.at[d - 1], along_x(d))

    def bx(d):
        part = wf.at[z, x, pl.ds(SPLIT, 192 - SPLIT)]
        return remote(part, part, bx_send.at[d - 1], bx_recv.at[d - 1], along_x(d))

    def bz(way, k):
        held = (z + (9 - k if way == 0 else 7 + k)) % 8
        part = wf.at[held, :, pl.ds(SPLIT, 192 - SPLIT)]
        i = way * 4 + k - 1
        return remote(part, part, bz_send.at[i], bz_recv.at[i], along_z(1 if way == 0 else 7))

    def ax_start(offset):
        for d in (1, 3, 2):
            ax(offset, d).start()

    def a_begin():
        spread_all().wait_recv()
        az(0, 1).start()
        az(1, 1).start()
        for d in (1, 3, 2):
            bx(d).start()
        ax_start(0)

    def b_begin():
        for d in (1, 3, 2):
            bx(d).wait_recv()
        bz(0, 1).start()
        bz(1, 1).start()

    def a_next(k):
        az(1, k).wait_recv()
        if k < 4:
            az(1, k + 1).start()
            az(0, k).wait_recv()
            if k < 3:
                az(0, k + 1).start()
            ax_start(8 - k)
        ax_start(k)

    def b_next(k):
        bz(0, k).wait_recv()
        if k < 4:
            bz(0, k + 1).start()
            bz(1, k).wait_recv()
            if k < 3:
                bz(1, k + 1).start()

    def lat_next(k):
        lat_step(k).wait_recv()
        if k < 2:
            lat_step(k + 1).start()
        share(k + 1).start()

    lat_pair().start()
    wk_in.wait()
    wv_in.wait()
    for d in (4, 2, 6):
        spread(d).start()
    a_begin()
    lat_pair().wait_recv()
    lat_step(0).start()
    lat_extra().start()
    share(0).start()
    a_next(1)
    b_begin()
    lat_next(0)
    for i in range(3):
        e_part(i).start()
    a_next(2)
    b_next(1)
    lat_next(1)
    a_next(3)
    lat_extra().wait_recv()
    lat_second().start()
    share(5).start()
    q_start(0)
    a_next(4)
    b_next(2)
    lat_next(2)
    lat_second().wait_recv()
    share(4).start()
    q_start(1)
    quarter_pair().start()
    b_next(3)
    q_start(2)
    q_start(3)
    e_in.wait()
    for i in range(3):
        e_part(i).wait_recv()
    powers = jnp.zeros((4 * ROWS, 64), F32)
    for level in range(-4, 5):
        powers = powers + jnp.where(ev[...] == level, F32(2.0**level), F32(0.0))
    pw[...] = powers.astype(BF)
    causal[...] = jnp.where(
        lax.broadcasted_iota(jnp.int32, (CHIP, CHIP), 1)
        <= lax.broadcasted_iota(jnp.int32, (CHIP, CHIP), 0),
        F32(0.0), F32(-BIG),
    )
    pltpu.make_async_copy(q2.at[:, my_rows], q2.at[:, my_rows], local_sem.at[4]).wait()
    for k in range(6):
        share(k).wait_recv()

    def chip_rows(slot):
        block = lat[slot // 2, slot % 2]
        return block.reshape(CHIP, WIDE)

    tail = jnp.concatenate([chip_rows(zh + k)[:, LATENT:] for k in range(11)], axis=0)
    kr[0, :, NOPE:] = tail
    kr[1, :, NOPE:] = tail
    lane = lax.broadcasted_iota(jnp.int32, (2 * CHIP, CHIP), 1)
    own_tail = jnp.concatenate([chip_rows(zh + k)[:, LATENT:] for k in (8, 10)], axis=0)
    noth[...] = jnp.where(lane < ROPE, F32(0.0), (own_tail.astype(F32) - 1.0) * F32(BIG))
    scale = F32(math.log2(math.e) / math.sqrt(NOPE + ROPE))

    def q_ready(r):
        for i in range(3):
            q_both(r, i).wait_recv()

    def far_a():
        for d in (1, 3, 2):
            ax_all(d).wait_recv()

    def quarter_next():
        quarter_pair().wait_recv()
        for d in (1, 3, 2):
            quarter_on(d).start()

    def quarter_done():
        for d in (1, 3, 2):
            quarter_on(d).wait_recv()

    events = {
        0: [lambda: q_ready(0)],
        1: [quarter_next, lambda: q_ready(1), far_a],
        3: [lambda: q_ready(2)],
        5: [lambda: q_ready(3), lambda: b_next(4)],
        7: [quarter_done],
    }

    def nt(left, right):
        return lax.dot_general(
            left, right, (((1,), (1,)), ((), ())), preferred_element_type=F32
        )

    def one_pair(t, carry):
        for when, todo in events.items():
            for event in todo:
                pl.when(t == when)(event)

        r = (t + 1) // 2 % 4
        zz = (zh + t) % 2
        j = (y // 2 + r) % 4 * 2 + zz
        pair = pair_of(j, a, c)

        @pl.when(r > 0)
        def _():
            start = pl.multiple_of(jnp.maximum(r - 1, 0) * 64, 64)
            wcur[...] = wf[pl.ds(zz * 4, 4), :, pl.ds(start, 64)].reshape(1024, 256)

        @pl.when(r == 0)
        def _():
            wcur[...] = wn[zz]

        latents = jnp.concatenate([chip_rows(zh + k)[:, :LATENT] for k in range(11)], axis=0)
        keys = jnp.dot(latents, wcur[:LATENT, :], preferred_element_type=F32).astype(BF)
        values = jnp.dot(latents, wcur[LATENT:, :], preferred_element_type=F32).astype(BF)
        kr[0, :, :NOPE] = keys[:, :NOPE]
        kr[1, :, :NOPE] = keys[:, NOPE:]
        pick = jnp.where(
            lax.broadcasted_iota(jnp.int32, (64, 384), 0)
            == 2 * pair + (lax.broadcasted_iota(jnp.int32, (64, 384), 1) >= 192).astype(jnp.int32),
            F32(1.0), F32(0.0),
        ).astype(BF)
        scaled = q2[j].astype(F32) * jnp.dot(pw[...], pick, preferred_element_type=F32)
        turned = pltpu.roll(scaled, 320, 1)
        queries = [
            jnp.concatenate(
                [scaled[:, :128], jnp.where(lane < ROPE, scaled[:, 128:256], noth[...])], axis=1
            ).astype(BF),
            jnp.concatenate(
                [turned[:, 128:256], jnp.where(lane < ROPE, turned[:, 256:], noth[...])], axis=1
            ).astype(BF),
        ]
        for h in range(2):
            both = nt(queries[h], kr[h, 256:WINDOW])
            first = nt(queries[h][:CHIP], kr[h, :256])
            last = nt(queries[h][CHIP:], kr[h, WINDOW:])
            scores = jnp.concatenate(
                [
                    jnp.concatenate([first, both[:CHIP]], axis=1),
                    jnp.concatenate([both[CHIP:], last], axis=1),
                ],
                axis=0,
            )
            mask = jnp.concatenate([causal[...], causal[...]], axis=0)
            scores = jnp.concatenate(
                [scores[:, : WINDOW - CHIP], scores[:, WINDOW - CHIP :] + mask], axis=1
            )
            largest = jnp.max(scores, axis=1, keepdims=True)
            weights = jnp.exp2((scores - largest) * scale)
            sums = jnp.sum(weights, axis=1, keepdims=True)
            weights = weights.astype(BF)
            for b in range(2):
                rows = slice(b * CHIP, (b + 1) * CHIP)
                weighted = jnp.dot(
                    weights[rows],
                    values[b * 256 : b * 256 + WINDOW, h * VDIM : (h + 1) * VDIM],
                    preferred_element_type=F32,
                )
                obuf[j, rows, h * VDIM : (h + 1) * VDIM] = (weighted / sums[rows]).astype(BF)
        columns = pl.ds(pl.multiple_of(pair * 256, 256), 256)
        for i in range(3):
            out_part(j, i, columns).start()
        out_ref[:, columns] = obuf[j, my_rows, :]
        return carry

    def out_part(j, i, columns):
        return remote(
            obuf.at[j, token_rows(team[i][0], team[i][1])], out_ref.at[:, columns],
            out_send.at[i * 8 + j], out_recv.at[i * 8 + j], team_at[i],
        )

    lax.fori_loop(0, 8, one_pair, 0)

    def finish(j, carry):
        for i in range(3):
            pair = pair_of(j, team[i][0], team[i][1])
            out_part(j, i, pl.ds(pl.multiple_of(pair * 256, 256), 256)).wait()
        return carry

    lax.fori_loop(0, 8, finish, 0)
    for i in range(3):
        e_part(i).wait_send()
        for r in range(4):
            q_both(r, i).wait_send()
    lat_pair().wait_send()
    lat_second().wait_send()
    lat_extra().wait_send()
    for k in range(3):
        lat_step(k).wait_send()
    for k in range(6):
        share(k).wait_send()
    quarter_pair().wait_send()
    spread_all().wait_send()
    for d in (1, 2, 3):
        quarter_on(d).wait_send()
        ax_all(d).wait_send()
        bx(d).wait_send()
    for k in range(1, 5):
        az(1, k).wait_send()
        bz(0, k).wait_send()
        if k < 4:
            az(0, k).wait_send()
            bz(1, k).wait_send()


def body(queries, exponents, latent, segments, key_weight, value_weight):
    documents = segments.reshape(1, ROWS)
    hbm = pl.BlockSpec(memory_space=pl.ANY)
    dma = pltpu.SemaphoreType.DMA
    return pl.pallas_call(
        kernel,
        out_shape=jax.ShapeDtypeStruct((ROWS, 8192), BF),
        in_specs=[hbm] * 6,
        out_specs=pl.BlockSpec(memory_space=pltpu.VMEM),
        scratch_shapes=[
            pltpu.VMEM((2, 1024, 256), BF),
            pltpu.VMEM((8, 4, 192, 256), BF),
            pltpu.VMEM((1024, 256), BF),
            pltpu.VMEM((8, 4 * ROWS, 384), BF),
            pltpu.VMEM((4 * ROWS, 64), jnp.int32),
            pltpu.VMEM((6, 2, 2, ROWS, WIDE), BF),
            pltpu.VMEM((ROWS, 576), BF),
            pltpu.VMEM((1, ROWS), jnp.int32),
            pltpu.VMEM((2, UNION, 256), BF),
            pltpu.VMEM((8, 4 * ROWS, 256), BF),
            pltpu.VMEM((4 * ROWS, 64), BF),
            pltpu.VMEM((2 * CHIP, CHIP), F32),
            pltpu.VMEM((CHIP, CHIP), F32),
            dma((6,)),
            dma((12,)), dma((12,)),
            dma((3,)), dma((3,)),
            dma((6,)), dma((6,)),
            dma((6,)), dma((6,)),
            dma((4,)), dma((4,)),
            dma((1,)), dma((1,)),
            dma((8,)), dma((8,)),
            dma((3,)), dma((3,)),
            dma((8,)), dma((8,)),
            dma((3,)), dma((3,)),
            dma((24,)), dma((24,)),
        ],
        compiler_params=pltpu.CompilerParams(
            collective_id=0, has_side_effects=True, vmem_limit_bytes=58 * 1024 * 1024
        ),
    )(queries, exponents, latent, documents, key_weight, value_weight)


def solution(mesh):
    both = ("blk", "head")
    placed = (
        P(both, None), P(both, None), P(both, None), P(both), P(None, "head"), P(None, "head"),
    )
    return jax.shard_map(
        body, mesh=mesh, in_specs=placed, out_specs=P(both, None), check_vma=False
    )
```
